256 devices in a mesh: group: 16 (over y, x), dev: 16 (over z, core).
Axes of the slice: x: 4, y: 4, z: 8, core: 2. Of those that a mesh axis runs over, the one named last changes fastest.
Arguments:
- points: float32 [3, 524288], P(None, ('group', 'dev')), may hold values from 0 to 1
- values: float32 [16, 524288], P(None, ('group', 'dev')), may hold values from -6 to 6
- counts: int32 [8192], P(('group', 'dev')), may hold values from 8 to 64, as said below
- leaf_basis: float32 [64, 524288], P(None, ('group', 'dev')), may hold values from -1 to 2
- local_pair: float32 [7936, 64, 128], P(('group', 'dev')), may hold values from -1 to 1
- chain_pair: float32 [256, 8, 64, 128], P(('group', 'dev')), may hold values from -1 to 1, as said below
- near_leaf: int32 [8192, 12], P(('group', 'dev')), may hold values from 0 to 31
- far_peer: int32 [8192, 4], P(('group', 'dev')), may hold values from 0 to 15, all different within a row; in each aligned block of 32 rows (0 to 31, 32 to 63, ...) at most 16 rows name the same one
- far_leaf: int32 [8192, 4], P(('group', 'dev')), may hold values from 0 to 31
- leaf_coupling: bfloat16 [4, 64, 524288], P(None, None, ('group', 'dev')), may hold values from -0.375 to 0.375
- group_far: int32 [16, 2], P('group'), may hold values from 0 to 14, all different within a row
- group_coupling: bfloat16 [2, 64, 1024], P(None, None, 'group'), may hold values from -0.75 to 0.75
Outputs:
- leaf_q: float32 [64, 524288], P(None, ('group', 'dev'))
- local_new: float32 [7936, 64, 128], P(('group', 'dev'))
- chain_new: float32 [256, 8, 64, 128], P(('group', 'dev'))
- product: float32 [16, 524288], P(None, ('group', 'dev'))
The draws below stay inside these ranges and needn't reach their ends.
Inputs may be any that keep to these rules, and one draw needn't show every extreme that they name: `counts`: the first leaf of every block has 64 live points, the second 64 // 8. chain_pair[s, j] is the same for all blocks s with the same s >> (j + 1). `far_peer`: the 4 offsets of one leaf differ; among the leaves of one block no offset appears more than 16 times, and some block of every draw has an offset that appears exactly 16 times. `group_far`: the 2 offsets of one subtree root differ.
All inputs are finite; a program needn't handle non-finite values.
Results may differ from the reference program's by a relative error of at most 0.0003.
Values sent between devices are 32-bit elements; how exact they have to be, the bound alone decides.
No kernel may reach another device: no remote copies, remote signals or barrier semaphores. Data moves between devices by JAX's collectives and lax.ppermute only.
A program may use at most 128 MiB of HBM per device.

```python
import math
import jax
import jax.numpy as jnp
import numpy as np
from jax import lax

K = 64
LEAF_DEV = 32
NV = 16
NEAR = 12
FAR = 4
GFAR = 2
SHARDS = 256
NL = 8192
NPTS = 524288
LPAR = 7936
DLEV = 4
UPL = 8
CAP = 16
N_GROUP = 16
N_DEV = 16


def pair_block(key, parents):
    jitter = 0.03 * jnp.clip(jax.random.normal(key, (parents, K, 2 * K), jnp.float32), -6.0, 6.0)
    row_ids = lax.broadcasted_iota(jnp.int32, (parents, K, 2 * K), 1)
    col_ids = lax.broadcasted_iota(jnp.int32, (parents, K, 2 * K), 2) % K
    return 0.70710678 * (jnp.where(row_ids == col_ids, 1.0, 0.0) + jitter)


def draw_counts(key, part):
    key = jax.random.fold_in(key, 5)
    drawn_counts = jax.random.randint(key, (NL,), K // 8, K + 1, dtype=jnp.int32)
    slot_ids = jnp.arange(NL, dtype=jnp.int32) % LEAF_DEV
    drawn_counts = jnp.where(slot_ids == 0, K, drawn_counts)
    return jnp.where(slot_ids == 1, K // 8, drawn_counts)


def draw_leaf_basis(key, part):
    key = jax.random.fold_in(key, 11)
    row_ids = lax.broadcasted_iota(jnp.int32, (K, NPTS), 0)
    col_ids = lax.broadcasted_iota(jnp.int32, (K, NPTS), 1) % K
    jitter = 0.03 * jnp.clip(jax.random.normal(key, (K, NPTS), jnp.float32), -6.0, 6.0)
    mixing = 0.7
    diagonal_part = jnp.where(row_ids == col_ids, 1.0, 0.0)
    band_part = jnp.where(row_ids + 1 == col_ids, 1.0, 0.0)
    return diagonal_part + mixing * band_part + jitter


def draw_local_pair(key, part):
    key = jax.random.fold_in(key, 17)
    return pair_block(key, LPAR)


def draw_chain_pair(key, part):
    key = jax.random.fold_in(key, 23)
    owner_ids = jnp.arange(SHARDS, dtype=jnp.int32)
    levels = []
    for level_index in range(UPL):
        node_pairs = pair_block(jax.random.fold_in(key, level_index), SHARDS // 2 ** (level_index + 1))
        levels.append(node_pairs[owner_ids >> level_index + 1])
    return jnp.stack(levels, axis=1)


def touch_ends(result, stream_key, low, largest):
    longest = result.shape.index(max(result.shape))
    spots = []
    for shift in (0, 1):
        where = [jax.random.randint(jax.random.fold_in(stream_key, axis), (), 0, length) for axis, length in enumerate(result.shape)]
        where[longest] = (where[longest] + shift) % result.shape[longest]
        spots.append(tuple(where))
    return result.at[spots[0]].set(low).at[spots[1]].set(largest)


def level_of(stream_key, shape, split, low, top_value):
    factor_of, own = 1.0, jax.random.fold_in(stream_key, 6)
    for position, shards_of in split:
        heights = jnp.exp(jax.random.uniform(jax.random.fold_in(own, position), (shards_of,), jnp.float32, low / len(split), top_value / len(split)))
        factor_of = factor_of * jnp.repeat(heights, shape[position] // shards_of).reshape([-1 if axis == position else 1 for axis in range(len(shape))])
    return factor_of


def distinct(rng, rows, number_of, top, lift):
    sequence = jax.random.permutation(jax.random.fold_in(rng, 1), number_of)
    pull = sequence
    for power in range(3):
        pull = pull * pull // number_of
    pull = pull * lift // number_of
    tickets = jax.random.randint(jax.random.fold_in(rng, 2), (rows, number_of), 0, 4096) + pull
    holders = jax.random.permutation(jax.random.fold_in(rng, 3), rows)[jnp.arange(number_of) % rows]
    tickets = jnp.where(jnp.arange(rows)[:, None] == holders[None, :], 1 << 14, tickets)
    score = tickets * number_of + jnp.arange(number_of)
    return lax.top_k(score.astype(jnp.int32), top)[1].astype(jnp.int32)


def routed_block(stream_key, own, number, rows, number_of, top, most, slope):
    sequence = jax.random.permutation(stream_key, number_of)
    packed, common = shares(number_of, rows * top, most, slope, True), shares(number_of, rows * top, most, slope, False)
    places = jnp.arange(number_of)

    def named(tallies, rotation):
        used = int((tallies > 0).sum())
        fixed = max(1, used // 4)
        moved = fixed + (places - fixed + rotation * (used - fixed)) % max(1, number_of - fixed)
        return jnp.zeros((number_of,), jnp.int32).at[sequence[jnp.where(places < fixed, places, moved)]].set(jnp.asarray(tallies, jnp.int32))

    tallies = jnp.where(number % 4 == 0, named(packed, number // 4), named(common, number - number // 4 - 1))
    mixed = jax.random.permutation(jax.random.fold_in(own, 3), number_of)
    giver, receiver = mixed[0:number_of // 2 * 2:2], mixed[1:number_of // 2 * 2:2]
    margin = jnp.minimum(tallies[giver] - 1, most - tallies[receiver]) // 2
    margin = jnp.where((giver == sequence[0]) | (receiver == sequence[0]) | (tallies[receiver] == 0), 0, jnp.maximum(margin, 0))
    moved = jax.random.randint(jax.random.fold_in(own, 4), (number_of // 2,), 0, 1 << 20) % (margin + 1)
    tallies = tallies.at[giver].add(-moved).at[receiver].add(moved)
    items = jnp.searchsorted(jnp.cumsum(tallies), jnp.arange(rows * top), side="right").astype(jnp.int32)
    listing = items.reshape(top, rows).T
    listing = listing[jax.random.permutation(jax.random.fold_in(own, 1), rows)]
    rotation = jax.random.randint(jax.random.fold_in(own, 2), (rows, 1), 0, top)
    return jnp.take_along_axis(listing, (jnp.arange(top)[None, :] + rotation) % top, axis=1)


def shares(number_of, total, most, slope, full):
    weights = [(1 << 20) // math.isqrt(rank ** slope) + 1 for rank in range(1, number_of + 1)]
    largest = most if full else min(most, max(-(-total // number_of), total * weights[0] // sum(weights)))
    least = 1 if total - largest >= number_of - 1 else 0
    holding, rest = [largest] + [least] * (number_of - 1), total - largest - least * (number_of - 1)
    while rest > 0:
        free = [i for i in range(1, number_of) if holding[i] < largest] or [i for i in range(1, number_of) if holding[i] < most]
        mass, budget = sum([weights[i] for i in free]), rest
        for i in free:
            addition = min(most - holding[i], max(1, budget * weights[i] // mass), rest)
            holding[i] = holding[i] + addition
            rest = rest - addition
    return np.array(holding)


def noise(rng, dims, width, reach, pieces=(), held_as=jnp.bfloat16):
    drawn = jax.random.normal(rng, dims, jnp.float32) * width
    if len(pieces) > 0:
        drawn = level_of(rng, dims, pieces, -0.22, 0.18) * drawn
    return jnp.clip(drawn, min=-reach, max=reach).astype(held_as)


def setup_inputs(seed: int = 0) -> dict:
    key_of = jax.random.split(jax.random.key(seed), 13)
    points = jnp.clip(1.0 * jax.random.uniform(key_of[0], (3, NPTS), jnp.float32) ** level_of(key_of[0], (3, NPTS), ((1, 256),), -0.2, 0.2), 0.0, 1.0)
    values = noise(key_of[1], (NV, NPTS), 1.0, 6.0, ((1, 256),), jnp.float32)
    counts = draw_counts(jax.random.fold_in(key_of[12], 71), 0)
    leaf_basis = draw_leaf_basis(jax.random.fold_in(key_of[12], 71), 0)
    local_pair = draw_local_pair(jax.random.fold_in(key_of[12], 71), 0)
    chain_pair = draw_chain_pair(jax.random.fold_in(key_of[12], 71), 0)
    near_leaf = touch_ends(jax.random.randint(key_of[6], (NL, NEAR), 0, LEAF_DEV), jax.random.fold_in(key_of[6], 1), 0, LEAF_DEV - 1).astype(jnp.int32)
    far_peer_keys = jax.random.split(jax.random.fold_in(key_of[7], 1), NL // LEAF_DEV)
    far_peer_turns = jax.random.permutation(jax.random.fold_in(key_of[7], 3), NL // LEAF_DEV)
    far_peer = jax.vmap(lambda own, number: routed_block(jax.random.fold_in(key_of[7], 2), own, number, LEAF_DEV, N_DEV, FAR, CAP, 2))(far_peer_keys, far_peer_turns).reshape((NL, FAR))
    far_leaf = touch_ends(jax.random.randint(key_of[8], (NL, FAR), 0, LEAF_DEV), jax.random.fold_in(key_of[8], 1), 0, LEAF_DEV - 1).astype(jnp.int32)
    leaf_coupling = noise(key_of[9], (FAR, K, NL * K), (K * FAR) ** -0.5, 0.375, ((2, 256),))
    group_far = distinct(key_of[10], N_GROUP, N_GROUP - 1, GFAR, 0)
    group_coupling = noise(key_of[11], (GFAR, K, N_GROUP * K), 0.125, 0.75, ((2, 16),))
    return {"points": points, "values": values, "counts": counts, "leaf_basis": leaf_basis, "local_pair": local_pair, "chain_pair": chain_pair, "near_leaf": near_leaf, "far_peer": far_peer, "far_leaf": far_leaf, "leaf_coupling": leaf_coupling, "group_far": group_far, "group_coupling": group_coupling}


highest = lax.Precision.HIGHEST
soft_square = 0.01

def factor(stacked):
    gram_matrix = jnp.einsum('nam,nbm->nab', stacked, stacked, precision=highest)
    lowers = jnp.linalg.cholesky(gram_matrix)
    identity = jnp.broadcast_to(jnp.eye(gram_matrix.shape[-1], dtype=jnp.float32), gram_matrix.shape)
    inverse = jax.scipy.linalg.solve_triangular(lowers, identity, lower=True)
    return (jnp.einsum('nab,nbm->nam', inverse, stacked, precision=highest), lowers)

def combine(left_lower, right_lower, pair_rows):
    rank_size = left_lower.shape[-1]
    stacked = jnp.concatenate([jnp.einsum('nab,nbc->nac', pair_rows[:, :, :rank_size], left_lower, precision=highest), jnp.einsum('nab,nbc->nac', pair_rows[:, :, rank_size:], right_lower, precision=highest)], axis=2)
    return factor(stacked)

def local_tree(stacked, pair_rows):
    leaf_count = stacked.shape[0]
    rank_size = stacked.shape[1]
    tree_depth = leaf_count.bit_length() - 1
    leaf_q, lowers = factor(stacked)
    new_levels = []
    for level_index in range(tree_depth - 1, -1, -1):
        parents = 2 ** level_index
        children = lowers.reshape(parents, 2, rank_size, rank_size)
        cluster_basis, lowers = combine(children[:, 0], children[:, 1], pair_rows[parents - 1:2 * parents - 1])
        new_levels.insert(0, cluster_basis)
    return (leaf_q, jnp.concatenate(new_levels, axis=0), lowers[0])

def climb_local(coeffs, new_pairs):
    tree_depth = (new_pairs.shape[0] + 1).bit_length() - 1
    vectors, rank_size = (coeffs.shape[1], coeffs.shape[2])
    for level_index in range(tree_depth - 1, -1, -1):
        parents = 2 ** level_index
        joined = coeffs.reshape(parents, 2, vectors, rank_size).transpose(0, 2, 1, 3).reshape(parents, vectors, 2 * rank_size)
        coeffs = jnp.einsum('nab,nvb->nva', new_pairs[parents - 1:2 * parents - 1], joined, precision=highest)
    return coeffs[0]

def descend_local(top_coeffs, new_pairs):
    tree_depth = (new_pairs.shape[0] + 1).bit_length() - 1
    vectors, rank_size = top_coeffs.shape
    coeffs = top_coeffs[None]
    for level_index in range(tree_depth):
        parents = 2 ** level_index
        spread = jnp.einsum('nva,nab->nvb', coeffs, new_pairs[parents - 1:2 * parents - 1], precision=highest)
        coeffs = spread.reshape(parents, vectors, 2, rank_size).transpose(0, 2, 1, 3).reshape(2 * parents, vectors, rank_size)
    return coeffs

def near_field(coords, near_rows, masked, near_scale):
    near_coords = coords[:, near_rows]
    leaf_count, near_count, rank_size = (near_coords.shape[1], near_coords.shape[2], near_coords.shape[3])
    square = jnp.zeros((leaf_count, near_count, rank_size, rank_size), jnp.float32)
    for axis_index in range(3):
        gap_value = coords[axis_index][:, None, :, None] - near_coords[axis_index][:, :, None, :]
        square = square + gap_value * gap_value
    kernel = 1.0 / jnp.sqrt(square + soft_square)
    return near_scale * jnp.einsum('pnxq,pnvq->pvx', kernel, masked[near_rows], precision=highest)

def reference(points, values, counts, leaf_basis, local_pair, chain_pair, near_leaf, far_peer, far_leaf, leaf_coupling, group_far, group_coupling):
    shards = N_GROUP * N_DEV
    shard_ids = jnp.arange(shards, dtype=jnp.int32)
    near_scale = float(K * NEAR) ** (-0.5)

    def live_rows(offset):
        live_counts = lax.dynamic_slice_in_dim(counts, offset, LEAF_DEV, 0)
        return (lax.broadcasted_iota(jnp.int32, (LEAF_DEV, K), 1) < live_counts[:, None]).astype(jnp.float32)

    def lower_part(shard_index):
        offset = shard_index * LEAF_DEV
        block_basis = lax.dynamic_slice_in_dim(leaf_basis, offset * K, LEAF_DEV * K, 1)
        stacked = block_basis.reshape(K, LEAF_DEV, K).transpose(1, 0, 2)
        pair_rows = lax.dynamic_slice_in_dim(local_pair, shard_index * (LEAF_DEV - 1), LEAF_DEV - 1, 0)
        leaf_q, new_pairs, root_lower = local_tree(stacked, pair_rows)
        block_values = lax.dynamic_slice_in_dim(values, offset * K, LEAF_DEV * K, 1)
        masked = block_values.reshape(NV, LEAF_DEV, K).transpose(1, 0, 2) * live_rows(offset)[:, None, :]
        coeffs = jnp.einsum('pax,pvx->pva', leaf_q, masked, precision=highest)
        return (leaf_q, new_pairs, root_lower, coeffs, climb_local(coeffs, new_pairs), masked)
    leaf_q, new_pairs, root_lowers, coeffs, root_coeffs, masked = lax.map(lower_part, shard_ids)
    lowers = root_lowers
    chain_levels = []
    for level_index in range(UPL):
        stride = 2 ** (level_index + 1)
        children = lowers.reshape(-1, 2, K, K)
        cluster_basis, lowers = combine(children[:, 0], children[:, 1], chain_pair[::stride, level_index])
        chain_levels.append(jnp.repeat(cluster_basis, stride, axis=0))
    chain_new = jnp.stack(chain_levels, axis=1)

    def halves(level_index):
        which_side = (shard_ids >> level_index & 1)[:, None, None]
        chain_q = chain_new[:, level_index]
        return jnp.where(which_side == 1, chain_q[:, :, K:], chain_q[:, :, :K])
    moving = root_coeffs
    for level_index in range(DLEV):
        moving = jnp.einsum('sab,svb->sva', halves(level_index), moving, precision=highest)
    group_coeffs = lax.optimization_barrier(jnp.sum(moving.reshape(N_GROUP, N_DEV, NV, K), axis=1))
    source_groups = (jnp.arange(N_GROUP, dtype=jnp.int32)[:, None] + 1 + group_far) % N_GROUP
    coupling = group_coupling.astype(jnp.float32).reshape(GFAR, K, N_GROUP, K)
    group_field = jnp.einsum('fjgi,gfvj->gvi', coupling, group_coeffs[source_groups], precision=highest)
    downward = group_field[shard_ids // N_DEV]
    for level_index in range(DLEV - 1, -1, -1):
        downward = jnp.einsum('sab,sva->svb', halves(level_index), downward, precision=highest)
    flat_coeffs = coeffs.reshape(shards * LEAF_DEV, NV, K)

    def upper_part(mapped_items):
        shard_index, block_q, block_pairs, top_coeffs, block_masked = mapped_items
        offset = shard_index * LEAF_DEV
        leaf_coeffs = descend_local(top_coeffs, block_pairs)
        peer_offset = lax.dynamic_slice_in_dim(far_peer, offset, LEAF_DEV, 0)
        source_leaf = lax.dynamic_slice_in_dim(far_leaf, offset, LEAF_DEV, 0)
        source_shard = shard_index // N_DEV * N_DEV + (shard_index % N_DEV + peer_offset) % N_DEV
        sources = flat_coeffs[source_shard * LEAF_DEV + source_leaf]
        block_coupling = lax.dynamic_slice_in_dim(leaf_coupling, offset * K, LEAF_DEV * K, 2)
        leaf_far = jnp.einsum('fjpi,pfvj->pvi', block_coupling.astype(jnp.float32).reshape(FAR, K, LEAF_DEV, K), sources, precision=highest)
        far_field = jnp.einsum('pax,pva->pvx', block_q, leaf_coeffs + leaf_far, precision=highest)
        coords = lax.dynamic_slice_in_dim(points, offset * K, LEAF_DEV * K, 1).reshape(3, LEAF_DEV, K)
        near_rows = lax.dynamic_slice_in_dim(near_leaf, offset, LEAF_DEV, 0)
        close_field = near_field(coords, near_rows, block_masked, near_scale)
        return ((far_field + close_field) * live_rows(offset)[:, None, :]).transpose(1, 0, 2)
    product = lax.map(upper_part, (shard_ids, leaf_q, new_pairs, downward, masked))
    leaf_out = leaf_q.transpose(2, 0, 1, 3).reshape(K, shards * LEAF_DEV * K)
    product = product.transpose(1, 0, 2, 3).reshape(NV, shards * LEAF_DEV * K)
    return (leaf_out, new_pairs.reshape(shards * (LEAF_DEV - 1), K, 2 * K), chain_new, product)
```

```python
import functools

import jax
import jax.numpy as jnp
from jax import lax
from jax.experimental import pallas as pl
from jax.experimental.pallas import tpu as pltpu
from jax.sharding import PartitionSpec as P

f32 = jnp.float32
bf16 = jnp.bfloat16
VMEM = pl.BlockSpec(memory_space=pltpu.VMEM)
SMEM = pl.BlockSpec(memory_space=pltpu.SMEM)
soft_square = 0.01
K = 64
LEAVES = 32
NV = 16


def split(x):
    hi = x.astype(bf16)
    return hi, (x - hi.astype(f32)).astype(bf16)


def contract(a, b, rhs_lanes):
    dims = (((1,), (1 if rhs_lanes else 0,)), ((), ()))
    return lax.dot_general(a, b, dims, preferred_element_type=f32)


def mm(a, b, rhs_lanes=False):
    ah, al = split(a)
    bh, bl = split(b)
    return contract(ah, bh, rhs_lanes) + (contract(ah, bl, rhs_lanes) + contract(al, bh, rhs_lanes))


def mm6(a, b, rhs_lanes=False):
    dims = (((1,), (1 if rhs_lanes else 0,)), ((), ()))
    return lax.dot_general(
        a, b, dims, preferred_element_type=f32, precision=lax.Precision.HIGHEST
    )


def left_lanes(shape):
    return lax.broadcasted_iota(jnp.int32, shape, 1) < K


def two_blocks(slab):
    left = left_lanes(slab.shape)
    return jnp.concatenate([jnp.where(left, slab, 0.0), jnp.where(left, 0.0, slab)], axis=0)


def pack(rows):
    half = rows.shape[0] // 2
    return jnp.concatenate([rows[:half], rows[half:]], axis=1)


def call(body, outs, *args, specs=None, scratch=(), vmem=48 << 20, flops=0, aliases=None):
    return pl.pallas_call(
        body,
        out_shape=[jax.ShapeDtypeStruct(s, d) for s, d in outs],
        in_specs=specs or [VMEM] * len(args),
        out_specs=[VMEM] * len(outs),
        scratch_shapes=list(scratch),
        compiler_params=pltpu.CompilerParams(vmem_limit_bytes=vmem),
        cost_estimate=pl.CostEstimate(flops=flops, bytes_accessed=1 << 20, transcendentals=0),
        name=body.func.__name__ if isinstance(body, functools.partial) else body.__name__,
    )(*args)


def upward(counts, basis, values, pair, gram_out, joined_out, masked_out, payload_out):
    lane = lax.broadcasted_iota(jnp.int32, (NV, 2 * K), 1)
    blocks, moments = {}, {}

    def keep(parent, block, moment):
        blocks[parent] = block
        moments[parent] = moment
        gram_out[parent * K : (parent + 1) * K, :] = block[:K] + block[K:]

    for p in range(LEAVES // 2):
        cols = slice(p * 2 * K, (p + 1) * 2 * K)
        live = (lane & K - 1) < jnp.where(lane < K, counts[2 * p], counts[2 * p + 1])
        masked = jnp.where(live, values[:, cols], 0.0)
        masked_out[:, cols] = masked
        stacked = two_blocks(basis[:, cols])
        both = mm6(jnp.concatenate([stacked, masked], axis=0), stacked, True)
        keep(LEAVES // 2 + p, both[: 2 * K], both[2 * K :])
    first = LEAVES // 2
    while first > 1:
        for a in range(first, 2 * first, 2):
            weights = pair[(a - 1) * K : (a + 1) * K, :]
            left = mm6(weights[:K], blocks[a])
            right = mm6(weights[K:], blocks[a + 1])
            joined_out[(a - 1) * K : a * K, :] = left
            joined_out[a * K : (a + 1) * K, :] = right
            both = mm6(
                jnp.concatenate([left, right, moments[a], moments[a + 1]], axis=0), weights, True
            )
            off = (lax.broadcasted_iota(jnp.int32, (2 * K, 2 * K), 1) // K) == (
                lax.broadcasted_iota(jnp.int32, (2 * K, 2 * K), 0) // K
            )
            keep(
                a // 2,
                jnp.where(off, both[: 2 * K], 0.0),
                jnp.where(lane < K, both[2 * K : 2 * K + NV], both[2 * K + NV :]),
            )
        first //= 2
    weights = pair[:K, :]
    left = mm6(weights, blocks[1])
    joined_out[:K, :] = left
    both = mm6(jnp.concatenate([left, moments[1]], axis=0), weights, True)
    root = both[:K]
    gram_out[:K, :] = jnp.concatenate([root, root], axis=1)
    payload_out[: K // 2, :] = pack(root)
    payload_out[K // 2 :, :] = pack(both[K:])


def chain_level(side, own, other, pair, gram_out, joined_out, payload_out):
    flip = jnp.full(own.shape, side[0], jnp.int32) == 1
    mine, theirs = own[...], other[...]
    low = jnp.where(flip, theirs, mine)
    high = jnp.where(flip, mine, theirs)
    low_turned = pltpu.roll(low, K, 1)
    high_turned = pltpu.roll(high, K, 1)
    half = K // 2
    left = left_lanes((half, 2 * K))
    slab = jnp.concatenate(
        [
            jnp.where(left, low[:half], high_turned[:half]),
            jnp.where(left, low_turned[:half], high[:half]),
        ],
        axis=0,
    )
    gram_out[...] = slab
    small = left_lanes((NV // 2, 2 * K))
    moment = jnp.concatenate(
        [
            jnp.where(small, low[half:], high_turned[half:]),
            jnp.where(small, low_turned[half:], high[half:]),
        ],
        axis=0,
    )
    weights = pair[...]
    joined = mm6(weights, two_blocks(slab))
    joined_out[...] = joined
    both = mm6(jnp.concatenate([joined, moment], axis=0), weights, True)
    payload_out[:half, :] = pack(both[:K])
    payload_out[half:, :] = pack(both[K:])


def inverse_factors(gram, out, rows, ratios):
    pairs = gram.shape[0] // K
    width = rows.shape[2]
    step = 4
    for i in range(K):
        turned = gram[pl.ds(i, pairs, stride=K), :].T
        rows[i, :, 0:pairs] = turned[:K]
        rows[i, :, pairs : 2 * pairs] = turned[K:]
    index = lax.broadcasted_iota(jnp.int32, (K, width), 0)
    for first in range(0, K, step):
        pivots, partial = [], []
        inside = (index >= first) & (index < first + step)
        for m in range(step):
            k = first + m
            row = rows[k]
            for n in range(m):
                scale = ratios[n, k : k + 1, :]
                row = jnp.where(index == first + n, 0.0, row) - scale * partial[n]
            diagonal = row[k : k + 1, :]
            ratio = row * (1.0 / diagonal)
            ratios[m] = ratio
            row = jnp.where(index == k, 1.0, row)
            partial.append(row)
            cleared = jnp.where(inside & (index > k), 0.0, row)
            pivots.append(cleared)
            done = jnp.where(index <= k, cleared * lax.rsqrt(diagonal), 0.0)
            turned = done.T
            out[pl.ds(k, pairs, stride=K), :] = jnp.concatenate(
                [turned[:pairs, :], turned[pairs : 2 * pairs, :]], axis=1
            )

        def trailing(i, carry):
            row = jnp.where(inside, 0.0, rows[i])
            for m in range(step):
                row = row - ratios[m, pl.ds(i, 1), :] * pivots[m]
            rows[i] = row
            return carry

        if first + step < K:
            lax.fori_loop(first + step, K, trailing, 0)


def factor_batch(gram):
    (out,) = call(
        inverse_factors,
        [(gram.shape, f32)],
        gram,
        scratch=[pltpu.VMEM((K, K, 2 * K), f32), pltpu.VMEM((4, K, 2 * K), f32)],
        flops=40_000_000,
    )
    return out


def bases(basis, masked, inverse, joined, q_out, new_out, coeff_out):
    for p in range(LEAVES // 2):
        cols = slice(p * 2 * K, (p + 1) * 2 * K)
        parent = LEAVES // 2 + p
        slab = mm(inverse[parent * K : (parent + 1) * K, :], two_blocks(basis[:, cols]))
        q_out[:, cols] = slab
        coeff_out[p * NV : (p + 1) * NV, :] = mm(masked[:, cols], two_blocks(slab), True)
    for h in range(LEAVES // 2):
        inner = []
        for n in (2 * h, 2 * h + 1):
            if n > 0:
                inner.append(
                    mm(
                        joined[(n - 1) * K : n * K, :],
                        two_blocks(inverse[n * K : (n + 1) * K, :]),
                        True,
                    )
                )
        if h == 0:
            new_out[:K, :] = mm(inverse[:K, :K], inner[0])
        else:
            new_out[(2 * h - 1) * K : (2 * h + 1) * K, :] = mm(
                two_blocks(inverse[h * K : (h + 1) * K, :]), jnp.concatenate(inner, axis=0)
            )


def near_fields(near, points, masked, out, places, columns, sources):
    left = left_lanes((8, 2 * K))
    wide = left_lanes((2 * NV, 2 * K))
    count = near.shape[0] // LEAVES
    scale = float(K * count) ** (-0.5)
    for p in range(LEAVES // 2):
        cols = slice(p * 2 * K, (p + 1) * 2 * K)
        place = jnp.concatenate([points[:, cols], jnp.zeros((5, 2 * K), f32)], axis=0)
        columns[p * 2 * K : (p + 1) * 2 * K, :] = place.T
        turned = pltpu.roll(place, K, 1)
        places[2 * p] = jnp.where(left, place, turned)
        places[2 * p + 1] = jnp.where(left, turned, place)
        high, low = split(masked[:, cols])
        both = jnp.concatenate([high.astype(f32), low.astype(f32)], axis=0)
        turned = pltpu.roll(both, K, 1)
        sources[2 * p] = jnp.where(wide, both, turned).astype(bf16)
        sources[2 * p + 1] = jnp.where(wide, turned, both).astype(bf16)

    def one(leaf):
        mine = columns[pl.ds(pl.multiple_of(leaf * K, K), K), :]
        own = [jnp.broadcast_to(mine[:, c : c + 1], (K, 2 * K)) for c in range(3)]
        total = jnp.zeros((NV, K), f32)
        for n in range(0, count, 2):
            first = near[leaf * count + n]
            second = near[leaf * count + n + 1]
            place = jnp.where(left, places[first], places[second])
            square = jnp.zeros((K, 2 * K), f32)
            for c in range(3):
                gap = own[c] - place[c : c + 1, :]
                square = square + gap * gap
            high, low = split(lax.rsqrt(square + soft_square))
            source = jnp.where(wide, sources[first].astype(f32), sources[second].astype(f32)).astype(bf16)
            part = contract(source, high, True)
            total = total + (part[:NV] + part[NV:] + contract(source[:NV], low, True))
        return total * scale

    def pair(p, carry):
        out[pl.ds(pl.multiple_of(p * NV, NV), NV), :] = jnp.concatenate(
            [one(2 * p), one(2 * p + 1)], axis=1
        )
        return carry

    lax.fori_loop(0, LEAVES // 2, pair, 0)


def root_coeffs(payload, inverse, out):
    half = K // 2
    small = payload[half:, :]
    moment = jnp.concatenate([small[:, :K], small[:, K:]], axis=0)
    out[...] = pack(mm(moment, inverse[:, :K], True))


def products(
    far_row, far_side, groups, sides, counts, spread, coupling, inverse_top, chain, pair, couplings, coeffs, basis, leaf_q, near, out
):
    field = jnp.zeros((NV, K), f32)
    for f in range(2):
        row = spread[pl.ds(pl.multiple_of(groups[f] * 8, 8), 8), :]
        source = jnp.concatenate([row[:, :K], row[:, K:]], axis=0)
        high, low = split(source)
        field = field + (contract(high, coupling[f], False) + contract(low, coupling[f], False))
    value = mm(field, inverse_top[:, :K])
    for j in range(3, -1, -1):
        both = mm(value, chain[j])
        flip = jnp.full((NV, K), sides[j], jnp.int32) == 1
        value = jnp.where(flip, both[:, K:], both[:, :K])
    slabs = {1: mm(value, pair[:K, :])}
    for a in range(2, LEAVES, 2):
        both = mm(two_blocks(slabs[a // 2]), pair[(a - 1) * K : (a + 1) * K, :])
        slabs[a] = both[:NV]
        slabs[a + 1] = both[NV:]
    lane = lax.broadcasted_iota(jnp.int32, (NV, 2 * K), 1)
    left = lane < K
    for p in range(LEAVES // 2):
        cols = slice(p * 2 * K, (p + 1) * 2 * K)
        lines = []
        for leaf in (2 * p, 2 * p + 1):
            halves = []
            for f in range(4):
                s = leaf * 4 + f
                row = coeffs[pl.ds(pl.multiple_of(far_row[s], NV), NV), :]
                turn = jnp.full((NV, 2 * K), far_side[s], jnp.int32) != (f & 1)
                halves.append(jnp.where(turn, pltpu.roll(row, K, 1), row))
            lines.append(
                jnp.concatenate(
                    [jnp.where(left, halves[0], halves[1]), jnp.where(left, halves[2], halves[3])],
                    axis=1,
                )
            )
        high, low = split(jnp.concatenate(lines, axis=0))
        weights = couplings[:, :, cols].reshape(4 * K, 2 * K)
        part = contract(high, weights, False) + contract(low, weights, False)
        leaf_field = jnp.where(left, part[:NV], part[NV:])
        total = mm(
            jnp.concatenate([slabs[LEAVES // 2 + p], leaf_field], axis=1),
            jnp.concatenate([two_blocks(basis[:, cols]), two_blocks(leaf_q[:, cols])], axis=0),
        )
        live = (lane & K - 1) < jnp.where(left, counts[2 * p], counts[2 * p + 1])
        out[:, cols] = jnp.where(live, total + near[p * NV : (p + 1) * NV, :], 0.0)


def chain_bases(inverse, joined, out):
    for j in range(8):
        inner = mm(joined[j * K : (j + 1) * K, :], two_blocks(inverse[j * K : (j + 1) * K, :]), True)
        out[j] = mm(inverse[(8 + j) * K : (9 + j) * K, :K], inner)


def swapped(x, axis, distance):
    return lax.ppermute(x, axis, [(i, i ^ 1 << distance) for i in range(lax.axis_size(axis))])


def unpacked(payload):
    half = K // 2
    return jnp.concatenate([payload[:half, :K], payload[:half, K:]], axis=0)


def per_device(
    points,
    values,
    counts,
    leaf_basis,
    local_pair,
    chain_pair,
    near_leaf,
    far_peer,
    far_leaf,
    leaf_coupling,
    group_far,
    group_coupling,
):
    dev_index = lax.axis_index("dev")
    group_index = lax.axis_index("group")
    pair = local_pair.reshape(31 * K, 2 * K)
    chain = chain_pair[0]
    gram, joined, masked, payload = call(
        upward,
        [((32 * K, 2 * K), f32), ((31 * K, 2 * K), f32), (values.shape, f32), ((40, 2 * K), f32)],
        counts,
        leaf_basis,
        values,
        pair,
        specs=[SMEM, VMEM, VMEM, VMEM],
        flops=1_000_000,
    )
    sides = [
        (dev_index >> j & 1) if j < 4 else (group_index >> (j - 4) & 1) for j in range(8)
    ]
    grams, joins, payloads = [], [], [payload]
    for j in range(8):
        other = swapped(payload, "dev", j) if j < 4 else swapped(payload, "group", j - 4)
        slab, join, payload = call(
            chain_level,
            [((K, 2 * K), f32), ((K, 2 * K), f32), ((40, 2 * K), f32)],
            sides[j].reshape(1),
            payload,
            other,
            chain[j],
            specs=[SMEM, VMEM, VMEM, VMEM],
            flops=1_000_000,
        )
        grams.append(slab)
        joins.append(join)
        payloads.append(payload)
    (near,) = call(
        near_fields,
        [((LEAVES // 2 * NV, 2 * K), f32)],
        near_leaf.reshape(-1),
        points,
        masked,
        specs=[SMEM, VMEM, VMEM],
        scratch=[
            pltpu.VMEM((LEAVES, 8, 2 * K), f32),
            pltpu.VMEM((LEAVES * K, 8), f32),
            pltpu.VMEM((LEAVES, 2 * NV, 2 * K), bf16),
        ],
        flops=40_000_000,
    )
    inverse = factor_batch(gram)
    leaf_q, new_pairs, coeffs = call(
        bases,
        [(leaf_basis.shape, f32), ((31 * K, 2 * K), f32), ((LEAVES // 2 * NV, 2 * K), f32)],
        leaf_basis,
        masked,
        inverse,
        joined,
        flops=40_000_000,
    )
    all_coeffs = lax.all_gather(coeffs, "dev", axis=0, tiled=True)
    top = unpacked(payloads[4])
    top_inverse = factor_batch(jnp.tile(top, (8, 2)))[:K]
    (root,) = call(root_coeffs, [((8, 2 * K), f32)], payloads[4], top_inverse)
    spread = lax.all_to_all(
        jnp.broadcast_to(root[None], (16, 8, 2 * K)), "group", 0, 0, tiled=True
    ).reshape(128, 2 * K)
    owners = [unpacked(payloads[j + 1]) for j in range(8)]
    chain_gram = jnp.concatenate(
        grams + [jnp.concatenate([o, o], axis=1) for o in owners], axis=0
    )
    chain_inverse = factor_batch(chain_gram)
    (chain_out,) = call(
        chain_bases, [((8, K, 2 * K), f32)], chain_inverse, jnp.concatenate(joins, axis=0)
    )
    source = (dev_index + far_peer) % 16 * (LEAVES // 2 * NV) + (far_leaf >> 1) * NV
    groups = ((group_index + 1 + group_far[0]) % 16).astype(jnp.int32)
    (product,) = call(
        products,
        [(values.shape, f32)],
        source.reshape(-1),
        (far_leaf & 1).reshape(-1),
        groups,
        jnp.stack(sides[:4]),
        counts,
        spread,
        group_coupling,
        top_inverse,
        chain[:4],
        pair,
        leaf_coupling,
        all_coeffs,
        leaf_basis,
        leaf_q,
        near,
        specs=[SMEM] * 5 + [VMEM] * 10,
        flops=40_000_000,
    )
    return (leaf_q, new_pairs.reshape(31, K, 2 * K), chain_out[None], product)


def solution(mesh):
    both = ("group", "dev")
    in_specs = (
        P(None, both),
        P(None, both),
        P(both),
        P(None, both),
        P(both, None, None),
        P(both, None, None, None),
        P(both, None),
        P(both, None),
        P(both, None),
        P(None, None, both),
        P("group", None),
        P(None, None, "group"),
    )
    out_specs = (
        P(None, both),
        P(both, None, None),
        P(both, None, None, None),
        P(None, both),
    )
    return jax.shard_map(
        per_device, mesh=mesh, in_specs=in_specs, out_specs=out_specs, check_vma=False
    )
```

```python
import functools

import jax
import jax.numpy as jnp
from jax import lax
from jax.experimental import pallas as pl
from jax.experimental.pallas import tpu as pltpu
from jax.sharding import PartitionSpec as P

f32 = jnp.float32
bf16 = jnp.bfloat16
VMEM = pl.BlockSpec(memory_space=pltpu.VMEM)
SMEM = pl.BlockSpec(memory_space=pltpu.SMEM)
soft_square = 0.01
K = 64
LEAVES = 32
NV = 16


def split(x):
    hi = x.astype(bf16)
    return hi, (x - hi.astype(f32)).astype(bf16)


def contract(a, b, rhs_lanes):
    dims = (((1,), (1 if rhs_lanes else 0,)), ((), ()))
    return lax.dot_general(a, b, dims, preferred_element_type=f32)


def mm(a, b, rhs_lanes=False):
    ah, al = split(a)
    bh, bl = split(b)
    return contract(ah, bh, rhs_lanes) + (contract(ah, bl, rhs_lanes) + contract(al, bh, rhs_lanes))


def mm6(a, b, rhs_lanes=False):
    dims = (((1,), (1 if rhs_lanes else 0,)), ((), ()))
    return lax.dot_general(
        a, b, dims, preferred_element_type=f32, precision=lax.Precision.HIGHEST
    )


gram_mm = mm


def left_lanes(shape):
    return lax.broadcasted_iota(jnp.int32, shape, 1) < K


def two_blocks(slab):
    left = left_lanes(slab.shape)
    return jnp.concatenate([jnp.where(left, slab, 0.0), jnp.where(left, 0.0, slab)], axis=0)


def pack(rows):
    half = rows.shape[0] // 2
    return jnp.concatenate([rows[:half], rows[half:]], axis=1)


def call(body, outs, *args, specs=None, scratch=(), after=(), us=0.02, vmem=16):
    given = len(args)

    def kernel(*refs):
        body(*refs[:given], *refs[given + len(after) :])

    return pl.pallas_call(
        kernel,
        out_shape=[jax.ShapeDtypeStruct(s, d) for s, d in outs],
        in_specs=(specs or [VMEM] * given) + [pl.BlockSpec(memory_space=pl.ANY)] * len(after),
        out_specs=[VMEM] * len(outs),
        scratch_shapes=list(scratch),
        compiler_params=pltpu.CompilerParams(vmem_limit_bytes=vmem << 20),
        cost_estimate=pl.CostEstimate(
            flops=int(us * 1e9), bytes_accessed=1 << 18, transcendentals=0
        ),
        name=body.func.__name__ if isinstance(body, functools.partial) else body.__name__,
    )(*args, *after)


def unpack(packed):
    return jnp.concatenate([packed[:, :K], packed[:, K:]], axis=0)


def side_by_side(low, high):
    left = left_lanes(low.shape)
    return jnp.concatenate(
        [
            jnp.where(left, low, pltpu.roll(high, K, 1)),
            jnp.where(left, pltpu.roll(low, K, 1), high),
        ],
        axis=0,
    )


def chosen(side, zero, one):
    return jnp.where(jnp.full(zero.shape, side, jnp.int32) == 1, one, zero)


def packed_level(side, own, other, weights):
    low, high = chosen(side, own, other), chosen(side, other, own)
    slab = side_by_side(low[:32], high[:32])
    joined = gram_mm(weights, two_blocks(slab))
    both = gram_mm(
        jnp.concatenate([joined, side_by_side(low[32:40], high[32:40])], axis=0), weights, True
    )
    return slab, joined, jnp.concatenate([pack(both[:K]), pack(both[K:])], axis=0)


def packed_share(side, own, weights):
    mine = chosen(side, weights[:, :K], weights[:, K:])
    inner = gram_mm(mine, unpack(own[:32]))
    both = gram_mm(jnp.concatenate([inner, unpack(own[32:40])], axis=0), mine, True)
    return jnp.concatenate([pack(both[:K]), pack(both[K:])], axis=0)


def upward(
    counts, sides, basis_in, values_in, pair_in, chain_in, gram_out, joined_out, masked_out, payload_out, share_out, basis, values, pair, chain, sems
):
    copies = [
        pltpu.make_async_copy(source, target, sems.at[n])
        for n, (source, target) in enumerate(
            ((values_in, values), (basis_in, basis), (pair_in, pair), (chain_in.at[pl.ds(0, K)], chain))
        )
    ]
    for copy in copies:
        copy.start()
    copies[0].wait()
    copies[1].wait()
    lane = lax.broadcasted_iota(jnp.int32, (NV, 2 * K), 1)
    blocks, moments = {}, {}

    def keep(parent, block, moment):
        blocks[parent] = block
        moments[parent] = moment
        gram_out[parent * K : (parent + 1) * K, :] = block[:K] + block[K:]

    for p in range(LEAVES // 2):
        cols = slice(p * 2 * K, (p + 1) * 2 * K)
        live = (lane & K - 1) < jnp.where(lane < K, counts[2 * p], counts[2 * p + 1])
        masked = jnp.where(live, values[:, cols], 0.0)
        masked_out[:, cols] = masked
        stacked = two_blocks(basis[:, cols])
        both = gram_mm(jnp.concatenate([stacked, masked], axis=0), stacked, True)
        keep(LEAVES // 2 + p, both[: 2 * K], both[2 * K :])
    copies[2].wait()
    copies[3].wait()
    first = LEAVES // 2
    while first > 1:
        for a in range(first, 2 * first, 2):
            weights = pair[(a - 1) * K : (a + 1) * K, :]
            left = gram_mm(weights[:K], blocks[a])
            right = gram_mm(weights[K:], blocks[a + 1])
            joined_out[(a - 1) * K : a * K, :] = left
            joined_out[a * K : (a + 1) * K, :] = right
            both = gram_mm(
                jnp.concatenate([left, right, moments[a], moments[a + 1]], axis=0), weights, True
            )
            off = (lax.broadcasted_iota(jnp.int32, (2 * K, 2 * K), 1) // K) == (
                lax.broadcasted_iota(jnp.int32, (2 * K, 2 * K), 0) // K
            )
            keep(
                a // 2,
                jnp.where(off, both[: 2 * K], 0.0),
                jnp.where(lane < K, both[2 * K : 2 * K + NV], both[2 * K + NV :]),
            )
        first //= 2
    weights = pair[:K, :]
    left = gram_mm(weights, blocks[1])
    joined_out[:K, :] = left
    both = gram_mm(jnp.concatenate([left, moments[1]], axis=0), weights, True)
    root = both[:K]
    gram_out[:K, :] = jnp.concatenate([root, root], axis=1)
    payload = jnp.concatenate([pack(root), pack(both[K:])], axis=0)
    payload_out[...] = payload
    share_out[...] = packed_share(sides[0], payload, chain[:K, :])


def two_levels(level, sides, own, near, far, farther, chain, slab_out, joined_out, *sends):
    start = own[:40, :]
    slab, joined, node = packed_level(sides[level], start, near[:40, :], chain[level * K : (level + 1) * K, :])
    slab_out[:K, :] = slab
    joined_out[:K, :] = joined
    rest = far[:40, :] + farther[:40, :]
    slab, joined, node = packed_level(sides[level + 1], node, rest, chain[(level + 1) * K : (level + 2) * K, :])
    slab_out[K:, :] = slab
    joined_out[K:, :] = joined
    if level < 6:
        share = packed_share(sides[level + 2], node, chain[(level + 2) * K : (level + 3) * K, :])
    if level == 0:
        sends[0][...] = node
        sends[1][...] = share
    elif level == 2:
        sends[0][...] = node
        sends[1][:32, :] = share[:32]
        sends[1][32:, :] = node
    elif level == 4:
        sends[0][:32, :] = node[:32]
        sends[1][:32, :] = share[:32]
        for send in sends:
            send[32:72, :] = start
            send[72:112, :] = near[...]
            send[112:152, :] = far[32:, :]
            send[152:, :] = farther[32:, :]
    else:
        sends[0][...] = node


def last_levels(
    sides, places, own, near, far, farther, chain, slabs0, slabs1, slabs2, joins0, joins1, joins2,
    gram_out, joined_out, moment_out, held, slabs, joins, top
):
    two_levels(6, sides, own, near, far, farther, chain, slabs, joins, top)
    for n, ref in enumerate((slabs0, slabs1, slabs2, slabs)):
        gram_out[2 * n * K : 2 * (n + 1) * K, :] = ref[...]
    for n, ref in enumerate((joins0, joins1, joins2, joins)):
        joined_out[2 * n * K : 2 * (n + 1) * K, :] = ref[...]
    for n, ref in enumerate((own, near, far, farther)):
        held[n * 160 : (n + 1) * 160, :] = ref[32:, :]
    sources = [held[pl.ds(pl.multiple_of(places[f] * 40, 8), 40), :] for f in range(2)]
    gram_out[8 * K : 9 * K, :] = side_by_side(top[:32, :], sources[0][:32])
    gram_out[9 * K : 10 * K, :] = side_by_side(sources[1][:32], sources[1][:32])
    for n in range(10, 16):
        gram_out[n * K : (n + 1) * K, :] = slabs[:K, :]
    moment_out[...] = side_by_side(sources[0][32:], sources[1][32:])


def inverse_factors(gram, out, rows, ratios):
    pairs = gram.shape[0] // K
    width = rows.shape[2]
    step, tile = 4, 8
    for i in range(K):
        turned = gram[pl.ds(i, pairs, stride=K), :].T
        rows[i, :, 0:pairs] = turned[:K]
        rows[i, :, pairs : 2 * pairs] = turned[K:]
    index = lax.broadcasted_iota(jnp.int32, (K, width), 0)
    near_index = lax.broadcasted_iota(jnp.int32, (tile, width), 0)
    for first in range(0, K, step):
        pivots, partial = [], []
        home = first // tile
        inside = (index >= first) & (index < first + step)
        for m in range(step):
            k = first + m
            row = rows[k]
            for n in range(m):
                scale = ratios[first + n, k : k + 1, :]
                row = jnp.where(index == first + n, 0.0, row) - scale * partial[n]
            diagonal = row[k : k + 1, :]
            ratios[k] = row * (1.0 / diagonal)
            row = jnp.where(index == k, 1.0, row)
            partial.append(row)
            pivots.append(jnp.where(inside & (index > k), 0.0, row))
            done = jnp.where(index <= k, row * lax.rsqrt(diagonal), 0.0)
            turned = done[:, : 2 * pairs].T
            out[pl.ds(k, pairs, stride=K), :] = jnp.concatenate(
                [turned[:pairs, :], turned[pairs:, :]], axis=1
            )
        start = first % tile
        cleared = (near_index >= start) & (near_index < start + step)
        for i in range(first + step, K):
            scales = [
                jnp.broadcast_to(ratios[first + m, i : i + 1, :], (tile, width))
                for m in range(step)
            ]
            for g in range(K // tile):
                if home < g < i // tile:
                    continue
                part = slice(g * tile, (g + 1) * tile)
                row = rows[i, part, :]
                if g == home:
                    row = jnp.where(cleared, 0.0, row)
                for m in range(step):
                    row = row - scales[m] * pivots[m][part]
                rows[i, part, :] = row


def factor_batch(gram, us=0.02):
    (out,) = call(
        inverse_factors,
        [(gram.shape, f32)],
        gram,
        scratch=[pltpu.VMEM((K, K, 2 * K), f32), pltpu.VMEM((K, K, 2 * K), f32)],
        us=us,
    )
    return out


def bases(basis, masked, inverse, q_out, coeff_out):
    for p in range(LEAVES // 2):
        cols = slice(p * 2 * K, (p + 1) * 2 * K)
        parent = LEAVES // 2 + p
        slab = mm(inverse[parent * K : (parent + 1) * K, :], two_blocks(basis[:, cols]))
        q_out[:, cols] = slab
        coeff_out[p * NV : (p + 1) * NV, :] = mm(masked[:, cols], two_blocks(slab), True)


def transfers(inverse, joined, new_out):
    for h in range(LEAVES // 2):
        inner = []
        for n in (2 * h, 2 * h + 1):
            if n > 0:
                inner.append(
                    mm(
                        joined[(n - 1) * K : n * K, :],
                        two_blocks(inverse[n * K : (n + 1) * K, :]),
                        True,
                    )
                )
        if h == 0:
            new_out[:K, :] = mm(inverse[:K, :K], inner[0])
        else:
            new_out[(2 * h - 1) * K : (2 * h + 1) * K, :] = mm(
                two_blocks(inverse[h * K : (h + 1) * K, :]), jnp.concatenate(inner, axis=0)
            )


def near_fields(start, stop, near, points, masked, out, places, columns, sources):
    left = left_lanes((8, 2 * K))
    wide = left_lanes((2 * NV, 2 * K))
    count = near.shape[0] // LEAVES
    scale = float(K * count) ** (-0.5)
    for p in range(LEAVES // 2):
        cols = slice(p * 2 * K, (p + 1) * 2 * K)
        place = jnp.concatenate([points[:, cols], jnp.zeros((5, 2 * K), f32)], axis=0)
        columns[p * 2 * K : (p + 1) * 2 * K, :] = place.T
        turned = pltpu.roll(place, K, 1)
        places[2 * p] = jnp.where(left, place, turned)
        places[2 * p + 1] = jnp.where(left, turned, place)
        high, low = split(masked[:, cols])
        both = jnp.concatenate([high.astype(f32), low.astype(f32)], axis=0)
        turned = pltpu.roll(both, K, 1)
        sources[2 * p] = jnp.where(wide, both, turned)
        sources[2 * p + 1] = jnp.where(wide, turned, both)

    def one(leaf):
        mine = columns[pl.ds(pl.multiple_of(leaf * K, K), K), :]
        own = [jnp.broadcast_to(mine[:, c : c + 1], (K, 2 * K)) for c in range(3)]
        total = jnp.zeros((2 * NV, 2 * K), f32)
        for n in range(0, count, 4):
            highs, lows, lines = [], [], []
            for step in (n, n + 2):
                first = near[leaf * count + step]
                second = near[leaf * count + step + 1]
                place = jnp.where(left, places[first], places[second])
                square = jnp.full((K, 2 * K), soft_square, f32)
                gaps = [own[c] - place[c : c + 1, :] for c in range(3)]
                square = gaps[0] * gaps[0] + gaps[1] * gaps[1] + gaps[2] * gaps[2] + soft_square
                high, low = split(lax.rsqrt(square))
                highs.append(high)
                lows.append(low)
                lines.append(jnp.where(wide, sources[first], sources[second]).astype(bf16))
            kernel = jnp.concatenate(
                [jnp.concatenate(highs, axis=1), jnp.concatenate(lows, axis=1)], axis=0
            )
            total = total + contract(jnp.concatenate(lines, axis=1), kernel, True)
        return (total[:NV, :K] + (total[NV:, :K] + total[:NV, K:])) * scale

    def pair(p, carry):
        out[pl.ds(pl.multiple_of((p - start) * NV, NV), NV), :] = jnp.concatenate(
            [one(2 * p), one(2 * p + 1)], axis=1
        )
        return carry

    lax.fori_loop(start, stop, pair, 0, unroll=4)


def chain_bases(sides, inverse, joined, out):
    inner = [
        mm(joined[j * K : (j + 1) * K, :], two_blocks(inverse[j * K : (j + 1) * K, :]), True)
        for j in range(8)
    ]
    for j in range(8):
        owner = inverse[(j + 1) * K : (j + 2) * K, :]
        mine = chosen(sides[j + 1], owner[:, :K], owner[:, K:]) if j < 7 else owner[:, :K]
        out[j] = mm(mine, inner[j])


def products(
    far_row, far_side, sides, counts, inverse, joined, moment, coupling, chain, pair, couplings, lower_half, upper_half, basis, leaf_q, near0, near1, out, chain_out, coeffs
):
    stacked_rows(lower_half, upper_half, coeffs)
    field = jnp.zeros((NV, K), f32)
    for f in range(2):
        found = inverse[8 * K : 9 * K, K:] if f == 0 else inverse[9 * K : 10 * K, :K]
        high, low = split(mm(moment[:, f * K : (f + 1) * K], found, True))
        field = field + (contract(high, coupling[f], False) + contract(low, coupling[f], False))
    owner = inverse[4 * K : 5 * K, :]
    value = mm(field, chosen(sides[4], owner[:, :K], owner[:, K:]))
    for j in range(3, -1, -1):
        both = mm(value, chain[j * K : (j + 1) * K, :])
        value = chosen(sides[j], both[:, :K], both[:, K:])
    slabs = {1: mm(value, pair[:K, :])}
    for a in range(2, LEAVES, 2):
        both = mm(two_blocks(slabs[a // 2]), pair[(a - 1) * K : (a + 1) * K, :])
        slabs[a] = both[:NV]
        slabs[a + 1] = both[NV:]
    chain_bases(sides, inverse, joined, chain_out)
    lane = lax.broadcasted_iota(jnp.int32, (NV, 2 * K), 1)
    left = lane < K
    for p in range(LEAVES // 2):
        cols = slice(p * 2 * K, (p + 1) * 2 * K)
        lines = []
        for leaf in (2 * p, 2 * p + 1):
            halves = []
            for f in range(4):
                s = leaf * 4 + f
                row = coeffs[pl.ds(pl.multiple_of(far_row[s], NV), NV), :]
                turn = jnp.full((NV, 2 * K), far_side[s], jnp.int32) != (f & 1)
                halves.append(jnp.where(turn, pltpu.roll(row, K, 1), row))
            lines.append(
                jnp.concatenate(
                    [jnp.where(left, halves[0], halves[1]), jnp.where(left, halves[2], halves[3])],
                    axis=1,
                )
            )
        high, low = split(jnp.concatenate(lines, axis=0))
        weights = couplings[:, :, cols].reshape(4 * K, 2 * K)
        part = contract(high, weights, False) + contract(low, weights, False)
        leaf_field = jnp.where(left, part[:NV], part[NV:])
        total = mm(
            jnp.concatenate([slabs[LEAVES // 2 + p], leaf_field], axis=1),
            jnp.concatenate([two_blocks(basis[:, cols]), two_blocks(leaf_q[:, cols])], axis=0),
        )
        live = (lane & K - 1) < jnp.where(left, counts[2 * p], counts[2 * p + 1])
        near = near0 if p < 8 else near1
        out[:, cols] = jnp.where(live, total + near[p % 8 * NV : (p % 8 + 1) * NV, :], 0.0)


def stacked_rows(first, second, out):
    rows = first.shape[0]
    out[:rows, :] = first[...]
    out[rows:, :] = second[...]


def join(first, second, after):
    shape = (2 * first.shape[0], first.shape[1])
    return call(stacked_rows, [(shape, f32)], first, second, after=after)[0]


def turned_ring(x, chips):
    size = lax.axis_size("dev")
    return lax.ppermute(
        x, "dev", [(i, (i + 2 * chips * (1 - 2 * (i & 1))) % size) for i in range(size)]
    )


def moved(x, axis, flip):
    return lax.ppermute(x, axis, [(i, i ^ flip) for i in range(lax.axis_size(axis))])


def per_device(
    points,
    values,
    counts,
    leaf_basis,
    local_pair,
    chain_pair,
    near_leaf,
    far_peer,
    far_leaf,
    leaf_coupling,
    group_far,
    group_coupling,
):
    dev_index = lax.axis_index("dev")
    group_index = lax.axis_index("group")
    pair = local_pair.reshape(31 * K, 2 * K)
    chain = chain_pair.reshape(8 * K, 2 * K)
    bits = jnp.arange(8, dtype=jnp.int32)
    sides = ((group_index * 16 + dev_index) >> bits) & 1
    near_ids = near_leaf.reshape(-1)
    slab = ((K, 2 * K), f32)
    gram, joined, masked, node, share = call(
        upward,
        [
            ((32 * K, 2 * K), f32),
            ((31 * K, 2 * K), f32),
            (values.shape, f32),
            ((40, 2 * K), f32),
            ((40, 2 * K), f32),
        ],
        counts,
        sides,
        leaf_basis,
        values,
        pair,
        chain,
        specs=[SMEM, SMEM] + [pl.BlockSpec(memory_space=pl.ANY)] * 4,
        scratch=[
            pltpu.VMEM(leaf_basis.shape, f32),
            pltpu.VMEM(values.shape, f32),
            pltpu.VMEM((31 * K, 2 * K), f32),
            pltpu.VMEM((K, 2 * K), f32),
            pltpu.SemaphoreType.DMA((4,)),
        ],
        vmem=56,
    )
    double = ((2 * K, 2 * K), f32)
    slabs, joins = [], []

    def climb(level, own, first, second, sends, after):
        axis, base = ("dev", 1 << level) if level < 4 else ("group", 1 << (level - 4))
        near = moved(first, axis, base)
        far = moved(second, axis, 2 * base)
        farther = moved(second, axis, 3 * base)
        body = functools.partial(two_levels, level)
        found = call(
            body,
            [double, double] + [((rows, 2 * K), f32) for rows in sends],
            sides,
            own,
            near,
            far,
            farther,
            chain,
            specs=[SMEM] + [VMEM] * 5,
            after=after,
        )
        slabs.append(found[0])
        joins.append(found[1])
        return found[2:]

    inverse = factor_batch(gram)
    node, share = climb(0, node, node, share, (40, 40), (inverse,))
    leaf_q, coeffs = call(
        bases,
        [(leaf_basis.shape, f32), ((LEAVES // 2 * NV, 2 * K), f32)],
        leaf_basis,
        masked,
        inverse,
        after=(share,),
    )
    (new_pairs,) = call(
        transfers, [((31 * K, 2 * K), f32)], inverse, joined, after=(coeffs,)
    )
    node, share = climb(2, node, node, share, (40, 72), (new_pairs,))
    coeffs = join(coeffs, turned_ring(coeffs, 2), (share,))

    def near_part(start, stop, after):
        return call(
            functools.partial(near_fields, start, stop),
            [(((stop - start) * NV, 2 * K), f32)],
            near_ids,
            points,
            masked,
            specs=[SMEM, VMEM, VMEM],
            scratch=[
                pltpu.VMEM((LEAVES, 8, 2 * K), f32),
                pltpu.VMEM((LEAVES * K, 8), f32),
                pltpu.VMEM((LEAVES, 2 * NV, 2 * K), f32),
            ],
            after=after,
        )[0]

    near0 = near_part(0, 8, (share,))
    send_near, send_far = climb(4, node, node, share, (192, 192), (near0,))
    coeffs = join(coeffs, turned_ring(coeffs, 4), (send_far,))
    near1 = near_part(8, 16, (send_far,))
    near = moved(send_near, "group", 4)
    far = moved(send_far, "group", 8)
    farther = moved(send_far, "group", 12)
    places = ((group_index + 1 + group_far[0]) % 16 ^ group_index).astype(jnp.int32)
    chain_gram, chain_joined, moment = call(
        last_levels,
        [((16 * K, 2 * K), f32), ((8 * K, 2 * K), f32), ((NV, 2 * K), f32)],
        sides,
        places,
        send_near,
        near,
        far,
        farther,
        chain,
        *slabs,
        *joins,
        specs=[SMEM] * 2 + [VMEM] * 11,
        scratch=[
            pltpu.VMEM((640, 2 * K), f32),
            pltpu.VMEM((2 * K, 2 * K), f32),
            pltpu.VMEM((2 * K, 2 * K), f32),
            pltpu.VMEM((40, 2 * K), f32),
        ],
        after=(near1,),
    )
    coeffs = join(coeffs, turned_ring(coeffs, 1), (moment,))
    chain_inverse = factor_batch(chain_gram, 6.5)
    others = moved(coeffs, "dev", 1)
    peer = (dev_index + far_peer) % 16
    core = peer & 1
    apart = (peer >> 1) - (dev_index >> 1)
    hops = jnp.where(core == 0, -apart, apart) & 7
    block = hops >> 1 | (hops & 1) << 2 | (core ^ (dev_index & 1)) << 3
    source = block * (LEAVES // 2 * NV) + (far_leaf >> 1) * NV
    product, chain_out = call(
        products,
        [(values.shape, f32), ((8, K, 2 * K), f32)],
        source.reshape(-1),
        (far_leaf & 1).reshape(-1),
        sides,
        counts,
        chain_inverse,
        chain_joined,
        moment,
        group_coupling,
        chain,
        pair,
        leaf_coupling,
        coeffs,
        others,
        leaf_basis,
        leaf_q,
        near0,
        near1,
        specs=[SMEM] * 4 + [VMEM] * 13,
        us=8.0,
        scratch=[pltpu.VMEM((16 * LEAVES // 2 * NV, 2 * K), f32)],
    )
    chain_out = chain_out.reshape(1, 8, K, 2 * K)
    return (leaf_q, new_pairs.reshape(31, K, 2 * K), chain_out, product)


def solution(mesh):
    both = ("group", "dev")
    in_specs = (
        P(None, both),
        P(None, both),
        P(both),
        P(None, both),
        P(both, None, None),
        P(both, None, None, None),
        P(both, None),
        P(both, None),
        P(both, None),
        P(None, None, both),
        P("group", None),
        P(None, None, "group"),
    )
    out_specs = (
        P(None, both),
        P(both, None, None),
        P(both, None, None, None),
        P(None, both),
    )
    return jax.shard_map(
        per_device, mesh=mesh, in_specs=in_specs, out_specs=out_specs, check_vma=False
    )
```
